256 devices in a mesh: group: 16 (over z_hi, y, core), mp: 16 (over x, z_lo).
Axes of the slice: x: 4, y: 4, z: 8 (z_hi: 2, z_lo: 4; z = z_hi * 4 + z_lo), core: 2. Of those that a mesh axis runs over, the one named last changes fastest.
Arguments:
- token_ids: int32 [512], replicated, may hold values from 0 to 76031
- page_ids: int32 [512], replicated, may hold values from 0 to 31, never falling along the last dimension, each value on 1 to 48 neighbouring positions
- tap_layer: int32 [32], replicated, may hold values from 0 to 1, as said below
- teacher_in: bfloat16 [512, 8192], P(None, 'mp'), may hold values from -60 to 60
- teacher_gain: bfloat16 [8192], P('mp'), may hold values from 0.25 to 1.75
- teacher_gate: bfloat16 [8192, 16384], P('mp', 'group'), may hold values from -0.0625 to 0.0625
- teacher_up: bfloat16 [8192, 16384], P('mp', 'group'), may hold values from -0.0625 to 0.0625
- teacher_down: bfloat16 [16384, 8192], P('group', 'mp'), may hold values from -0.375 to 0.375
- student_embed: bfloat16 [76032, 3584], P('mp', 'group'), may hold values from -25 to 25
- student_gain: bfloat16 [3584], P('group'), may hold values from 0.25 to 1.75
- student_gate: bfloat16 [3584, 10240], P('group', 'mp'), may hold values from -0.09375 to 0.09375
- student_up: bfloat16 [3584, 10240], P('group', 'mp'), may hold values from -0.09375 to 0.09375
- student_down: bfloat16 [10240, 3584], P('mp', 'group'), may hold values from -0.0625 to 0.0625
- projection: bfloat16 [3584, 8192], P('group', 'mp'), may hold values from -0.09375 to 0.09375
Outputs:
- loss: float32 [], replicated
- grad_gate: float32 [3584, 10240], P('group', 'mp')
- grad_up: float32 [3584, 10240], P('group', 'mp')
- grad_down: float32 [10240, 3584], P('mp', 'group')
- grad_proj: float32 [3584, 8192], P('group', 'mp')
The draws below stay inside these ranges and needn't reach their ends.
Inputs may be any that keep to these rules, and one draw needn't show every extreme that they name: `page_ids`: pages are runs of consecutive tokens numbered in order from 0; each of the 32 pages holds 1 to 48 tokens. `tap_layer`: 0 matches a page to the teacher layer's input, 1 to its output; both values occur.
All inputs are finite; a program needn't handle non-finite values.
Results may differ from the reference program's by a relative error of at most 0.04.
Values may be sent and summed in bfloat16 or wider, within the bound.
No kernel may reach another device: no remote copies, remote signals or barrier semaphores. Data moves between devices by JAX's collectives and lax.ppermute only.
A program may use at most 64 MiB of HBM per device.

```python
import math
import jax
import jax.numpy as jnp
import numpy as np
from jax import lax

DT = 8192
FT = 16384
DS = 3584
FS = 10240
VOCAB = 76032
TOKENS = 512
PAGE_MOST = 48
PAGES = 32
N_GROUP = 16
N_MP = 16


def scaled_field(key, rows, cols, row_low, row_high, rise, scale, row_rise):
    base_key, row_key, col_key = jax.random.split(key, 3)
    row_scale = jnp.exp(jax.random.uniform(row_key, (rows, 1), minval=math.log(row_low), maxval=math.log(row_high)))
    row_scale = row_scale * (row_rise ** (jnp.arange(rows, dtype=jnp.float32) / rows - 1.0))[:, None]
    col_scale = jnp.exp(jax.random.uniform(col_key, (1, cols), minval=-0.3, maxval=0.3))
    col_scale = col_scale * (rise ** (jnp.arange(cols, dtype=jnp.float32) / cols))[None, :]
    bell = jnp.clip(jax.random.normal(base_key, (rows, cols)), -4.0, 4.0)
    base = bell
    return scale * base * row_scale * col_scale


def draw_teacher_in(key, part):
    key = jax.random.fold_in(key, 11)
    values = scaled_field(key, TOKENS, DT, 1.0, 10.0, 10.0, 0.1, 3.0)
    return values.astype(jnp.bfloat16)


def draw_student_embed(key, part):
    key = jax.random.fold_in(key, 17)
    values = scaled_field(key, VOCAB, DS, 0.5, 5.0, 3.0, 0.3, 1.0)
    return values.astype(jnp.bfloat16)


def draw_tap_layer(key, part):
    key = jax.random.fold_in(key, 23)
    picks = jax.random.randint(key, (PAGES,), 0, 2, dtype=jnp.int32)
    return picks.at[0].set(1 - picks[1]).astype(jnp.int32)


def place_ends(entries, rng, low, largest):
    place = [jax.random.randint(jax.random.fold_in(rng, axis), (), 0, length) for axis, length in enumerate(entries.shape)]
    main_axis = entries.shape.index(max(entries.shape))
    neighbour = place[:main_axis] + [(place[main_axis] + 1) % entries.shape[main_axis]] + place[main_axis + 1:]
    return entries.at[tuple(place)].set(low).at[tuple(neighbour)].set(largest)


def block_scale(own_key, dims, shards, low, high):
    level, own = 1.0, jax.random.fold_in(own_key, 6)
    for dim, parts in shards:
        heights = jnp.exp(jax.random.uniform(jax.random.fold_in(own, dim), (parts,), jnp.float32, low / len(shards), high / len(shards)))
        level = level * jnp.repeat(heights, dims[dim] // parts).reshape([-1 if axis == dim else 1 for axis in range(len(dims))])
    return level


def ranked_wide(rng, shape, count, lean):
    weights = [min(1 << octave, count + 1 - (1 << octave)) * (1 << 20) // math.isqrt((1 << octave) ** lean) + 1 for octave in range((count + 1).bit_length()) if 1 << octave <= count]
    scale = 1 + sum(weights) // (1 << 30)
    listing = np.cumsum(np.array([max(1, weight // scale) for weight in weights]))
    pick = jax.random.randint(jax.random.fold_in(rng, 1), shape, 0, int(listing[len(weights) - 1]))
    start = jnp.left_shift(1, jnp.searchsorted(jnp.asarray(listing, jnp.int32), pick, side="right").astype(jnp.int32))
    rank = start - 1 + jax.random.randint(jax.random.fold_in(rng, 4), shape, 0, 1 << 30) % jnp.minimum(start, count + 1 - start)
    return jax.random.permutation(jax.random.fold_in(rng, 2), count)[rank].astype(jnp.int32)


def profile(number_of, total, most, skew):
    loads = [(1 << 20) // math.isqrt(rank ** skew) + 1 for rank in range(2, number_of + 1)]
    rest, holding = total - most - (number_of - 1), [1] * (number_of - 1)
    while rest > 0:
        free = [i for i in range(number_of - 1) if holding[i] < most]
        whole, left = sum([loads[i] for i in free]), rest
        for i in free:
            extra = min(most - holding[i], max(1, left * loads[i] // whole), rest)
            holding[i] = holding[i] + extra
            rest = rest - extra
    return np.array([most] + holding)


def ragged(own_key, count, total, limit, skew):
    if count == 2:
        one = jax.random.randint(own_key, (), max(1, total - limit), min(limit, total - 1) + 1)
        return jnp.stack([one, total - one])
    sizes = jnp.asarray(profile(count, total, limit, skew), jnp.int32)
    couples = (count - 1) // 2
    giver, receiver = sizes[1:1 + 2 * couples:2], sizes[2:2 + 2 * couples:2]
    margin = jnp.minimum(giver - 1, limit - receiver)
    passed = jax.random.randint(jax.random.fold_in(own_key, 1), (couples,), 0, 1 << 20) % (margin + 1)
    sizes = sizes.at[1:1 + 2 * couples:2].set(giver - passed).at[2:2 + 2 * couples:2].set(receiver + passed)
    return sizes[jax.random.permutation(jax.random.fold_in(own_key, 2), count)]


def scatter_about(rng, dims, scale, limit, shards=(), kind=jnp.bfloat16):
    level = block_scale(rng, dims, shards, -0.22, 0.18) if shards else 1.0
    drawn = jax.random.normal(rng, dims, jnp.float32) * scale * level
    return jnp.minimum(jnp.maximum(drawn, -limit), limit).astype(kind)


def setup_inputs(seed: int = 0) -> dict:
    streams_of = jax.random.split(jax.random.key(seed), 15)
    token_ids = place_ends(ranked_wide(streams_of[0], (TOKENS,), VOCAB, 2), jax.random.fold_in(streams_of[0], 3), 0, VOCAB - 1).astype(jnp.int32)
    page_ids = jnp.searchsorted(jnp.cumsum(ragged(streams_of[1], PAGES, TOKENS, PAGE_MOST, 1)), jnp.arange(TOKENS), side="right").astype(jnp.int32)
    tap_layer = draw_tap_layer(jax.random.fold_in(streams_of[14], 71), 0)
    teacher_in = draw_teacher_in(jax.random.fold_in(streams_of[14], 71), 0)
    teacher_gain = jnp.clip(1.0 + 0.15 * jax.random.normal(streams_of[4], (DT,), jnp.float32), 0.25, 1.75).astype(jnp.bfloat16)
    teacher_gate = scatter_about(streams_of[5], (DT, FT), DT ** -0.5, 0.0625, ((0, 16), (1, 16)))
    teacher_up = scatter_about(streams_of[6], (DT, FT), DT ** -0.5, 0.0625, ((0, 16), (1, 16)))
    teacher_down = scatter_about(streams_of[7], (FT, DT), (FT // 64) ** -0.5, 0.375, ((0, 16), (1, 16)))
    student_embed = draw_student_embed(jax.random.fold_in(streams_of[14], 71), 0)
    student_gain = jnp.clip(1.0 + 0.15 * jax.random.normal(streams_of[9], (DS,), jnp.float32), 0.25, 1.75).astype(jnp.bfloat16)
    student_gate = scatter_about(streams_of[10], (DS, FS), DS ** -0.5, 0.09375, ((0, 16), (1, 16)))
    student_up = scatter_about(streams_of[11], (DS, FS), DS ** -0.5, 0.09375, ((0, 16), (1, 16)))
    student_down = scatter_about(streams_of[12], (FS, DS), FS ** -0.5, 0.0625, ((0, 16), (1, 16)))
    projection = scatter_about(streams_of[13], (DS, DT), DS ** -0.5, 0.09375, ((0, 16), (1, 16)))
    return {"token_ids": token_ids, "page_ids": page_ids, "tap_layer": tap_layer, "teacher_in": teacher_in, "teacher_gain": teacher_gain, "teacher_gate": teacher_gate, "teacher_up": teacher_up, "teacher_down": teacher_down, "student_embed": student_embed, "student_gain": student_gain, "student_gate": student_gate, "student_up": student_up, "student_down": student_down, "projection": projection}


EPS = 1e-06

def rms_scale(values, gain, width):
    wide = values.astype(jnp.float32)
    squares = lax.optimization_barrier(jnp.sum(wide * wide, axis=1))
    return (wide * lax.rsqrt(squares / width + EPS)[:, None] * gain.astype(jnp.float32)).astype(jnp.bfloat16)

def blocked_product(left, right, blocks):
    size = left.shape[1] // blocks

    def add_block(total, index):
        start = (index * size).astype(jnp.int32)
        left_part = lax.dynamic_slice_in_dim(left, start, size, 1)
        right_part = lax.dynamic_slice_in_dim(right, start, size, 0)
        term = jnp.dot(left_part, right_part, preferred_element_type=jnp.float32).astype(jnp.bfloat16)
        term = lax.optimization_barrier(term)
        return (total + term.astype(jnp.float32), None)
    initial = jnp.zeros((left.shape[0], right.shape[1]), jnp.float32)
    total, _ = lax.scan(add_block, initial, jnp.arange(blocks, dtype=jnp.int32))
    return total

def silu_parts(values):
    sigmoid = jax.nn.sigmoid(values)
    return (values * sigmoid, sigmoid * (1.0 + values * (1.0 - sigmoid)))

def reference(token_ids, page_ids, tap_layer, teacher_in, teacher_gain, teacher_gate, teacher_up, teacher_down, student_embed, student_gain, student_gate, student_up, student_down, projection):
    teacher_normed = rms_scale(teacher_in, teacher_gain, DT)
    teacher_gate_sum = blocked_product(teacher_normed, teacher_gate, N_MP)
    teacher_up_sum = blocked_product(teacher_normed, teacher_up, N_MP)
    teacher_active, _ = silu_parts(teacher_gate_sum)
    teacher_hidden = (teacher_active * teacher_up_sum).astype(jnp.bfloat16)
    teacher_out = (teacher_in.astype(jnp.float32) + jnp.dot(teacher_hidden, teacher_down, preferred_element_type=jnp.float32)).astype(jnp.bfloat16)
    tapped = jnp.take(tap_layer, page_ids)
    target = jnp.where((tapped == 1)[:, None], teacher_out, teacher_in)
    student_in = jnp.take(student_embed, token_ids, axis=0)
    student_normed = rms_scale(student_in, student_gain, DS)
    gate_sum = blocked_product(student_normed, student_gate, N_GROUP)
    up_sum = blocked_product(student_normed, student_up, N_GROUP)
    active, slope = silu_parts(gate_sum)
    student_hidden = (active * up_sum).astype(jnp.bfloat16)
    student_out = (student_in.astype(jnp.float32) + jnp.dot(student_hidden, student_down, preferred_element_type=jnp.float32)).astype(jnp.bfloat16)
    predicted = jnp.dot(student_out, projection, preferred_element_type=jnp.float32)
    member = (page_ids[:, None] == jnp.arange(PAGES, dtype=jnp.int32)[None, :]).astype(jnp.float32)
    counts = lax.optimization_barrier(jnp.sum(member, axis=0))
    weight = 1.0 / (PAGES * jnp.take(counts, page_ids))
    difference = predicted - target.astype(jnp.float32)
    loss = jnp.sum(weight[:, None] * difference * difference) / DT
    pred_grad = (TOKENS / 16 * weight[:, None] * difference).astype(jnp.bfloat16)
    grad_proj = jnp.dot(student_out.T, pred_grad, preferred_element_type=jnp.float32)
    out_grad = jnp.dot(pred_grad, projection.T, preferred_element_type=jnp.float32).astype(jnp.bfloat16)
    grad_down = jnp.dot(student_hidden.T, out_grad, preferred_element_type=jnp.float32)
    hidden_grad = blocked_product(out_grad, student_down.T, N_GROUP)
    gate_grad = (hidden_grad * up_sum * slope).astype(jnp.bfloat16)
    up_grad = (hidden_grad * active).astype(jnp.bfloat16)
    grad_gate = jnp.dot(student_normed.T, gate_grad, preferred_element_type=jnp.float32)
    grad_up = jnp.dot(student_normed.T, up_grad, preferred_element_type=jnp.float32)
    return (loss, grad_gate, grad_up, grad_down, grad_proj)
```

```python
import jax
import jax.numpy as jnp
from jax import lax
from jax.sharding import Mesh, PartitionSpec as P

DT = 8192
DS = 3584

EPS = 1e-06

F32 = jnp.float32
BF16 = jnp.bfloat16
GROUP = ("zh", "y", "c")
MODEL = ("x", "zl")
SWAP = [(0, 1), (1, 0)]
LANES = 256


def silu_parts(values):
    sigmoid = jax.nn.sigmoid(values)
    return (values * sigmoid, sigmoid * (1.0 + values * (1.0 - sigmoid)))


def product(left, right):
    return jnp.dot(left, right, preferred_element_type=F32)


def transpose_product(left, right):
    return lax.dot_general(left, right, (((0,), (0,)), ((), ())), preferred_element_type=F32)


def product_transposed(left, right):
    return lax.dot_general(left, right, (((1,), (1,)), ((), ())), preferred_element_type=F32)


def swap(values, axis):
    return lax.ppermute(values, axis, SWAP)


def exchange(values, axis):
    return lax.all_to_all(values, axis, 0, 0, tiled=True)


def spread(values, axis):
    count = lax.axis_size(axis)
    copies = jnp.broadcast_to(values[None], (count,) + values.shape)
    return exchange(copies.reshape((count * values.shape[0],) + values.shape[1:]), axis)


def sum_scatter(values, axis):
    count = lax.axis_size(axis)
    parts = exchange(values, axis)
    parts = parts.reshape((count, values.shape[0] // count) + values.shape[1:])
    return jnp.sum(parts.astype(F32), axis=0)


def group_sum(mine, other):
    received = swap(other.astype(BF16), "c")
    pair = (mine + received.astype(F32)).astype(BF16)
    total = sum_scatter(pair, "y")
    return total + swap(total.astype(BF16), "zh").astype(F32)


def group_rows(values):
    mine = spread(values, "y")
    return mine, swap(mine, "c")


def two_parts(values):
    high = lax.reduce_precision(values, 8, 7)
    return jnp.stack([high, values - high], axis=1).astype(BF16)


def widen(values, extra):
    rows = values.shape[0]
    left = LANES - values.shape[1] - extra.shape[1]
    return jnp.concatenate([values, extra, jnp.zeros((rows, left), BF16)], axis=1)


def shards(
    token_ids,
    page_ids,
    tap_layer,
    teacher_in,
    teacher_gain,
    teacher_gate,
    teacher_up,
    teacher_down,
    student_embed,
    student_gain,
    student_gate,
    student_up,
    student_down,
    projection,
):
    core = lax.axis_index("c")
    tokens, teacher_width = teacher_in.shape
    half = tokens // 2
    block = half // lax.axis_size("y")
    student_width = student_gain.shape[0]

    def halves_first(values):
        turned = jnp.concatenate([values[half:], values[:half]], axis=0)
        return jnp.where(core == 0, values, turned)

    ids = halves_first(token_ids)
    pages_of = halves_first(page_ids)
    teacher_rows = halves_first(teacher_in)
    row_start = lax.axis_index("y") * block

    pages = tap_layer.shape[0]
    member = pages_of[:, None] == jnp.arange(pages, dtype=jnp.int32)[None, :]
    counts = jnp.sum(member.astype(F32), axis=0)
    page_weight = 1.0 / (pages * counts)
    token_weight = jnp.sum(jnp.where(member, page_weight[None, :], 0.0), axis=1)
    token_tap = jnp.sum(jnp.where(member, tap_layer[None, :], 0), axis=1) == 1
    weight = lax.dynamic_slice_in_dim(token_weight, row_start, block, 0)[:, None]
    tap_scale = jnp.where(token_tap, 1.0, 0.0)[:, None]

    vocab_rows = student_embed.shape[0]
    local_ids = ids - lax.axis_index(MODEL) * vocab_rows
    inside = (local_ids >= 0) & (local_ids < vocab_rows)
    picked = jnp.take(student_embed, jnp.clip(local_ids, 0, vocab_rows - 1), axis=0)
    picked = jnp.where(inside[:, None], picked, jnp.zeros((), BF16))
    teacher_float = teacher_rows.astype(F32)
    teacher_square = jnp.sum(teacher_float * teacher_float, axis=1)
    first = sum_scatter(widen(picked, two_parts(teacher_square)), MODEL)
    student_in = first[:, :student_width]
    teacher_total = first[:, student_width] + first[:, student_width + 1]
    student_square = jnp.sum(student_in * student_in, axis=1)
    scaled = (student_in * student_gain.astype(F32)).astype(BF16)
    student_all = spread(
        widen(scaled, jnp.concatenate([two_parts(student_square), two_parts(teacher_total)], axis=1)),
        MODEL,
    )
    student_scaled = student_all[:, :student_width]
    teacher_square_all = student_all[:, student_width + 2].astype(F32) + student_all[
        :, student_width + 3
    ].astype(F32)

    teacher_scaled = (teacher_float * teacher_gain.astype(F32)).astype(BF16)
    teacher_both = jnp.concatenate([teacher_gate, teacher_up], axis=1)
    teacher_partial = product(teacher_scaled, teacher_both).astype(BF16)
    teacher_sums = sum_scatter(sum_scatter(teacher_partial, "x").astype(BF16), "zl")
    model_rows = tokens // lax.axis_size(MODEL)
    teacher_scale = lax.rsqrt(teacher_total / DT + EPS)[:, None]
    hidden_width = teacher_gate.shape[1]
    teacher_active, _ = silu_parts(teacher_sums[:, :hidden_width] * teacher_scale)
    teacher_share = (teacher_active * (teacher_sums[:, hidden_width:] * teacher_scale)).astype(BF16)
    teacher_hidden = spread(spread(teacher_share, "zl"), "x")

    columns = student_gate.shape[1]
    student_both = jnp.concatenate([student_gate, student_up], axis=1)
    depth = LANES - student_width
    carry = (jnp.arange(depth)[:, None] < 2) & (jnp.arange(128)[None, :] == 0)
    student_both = jnp.concatenate(
        [
            jnp.concatenate([student_both, jnp.zeros((student_width, 128), BF16)], axis=1),
            jnp.concatenate([jnp.zeros((depth, 2 * columns), BF16), carry.astype(BF16)], axis=1),
        ],
        axis=0,
    )
    sums = group_sum(
        product(student_all[:half], student_both), product(student_all[half:], student_both)
    )
    student_scale = lax.rsqrt(sums[:, 2 * columns : 2 * columns + 1] / DS + EPS)
    up_sum = sums[:, columns : 2 * columns] * student_scale
    active, slope = silu_parts(sums[:, :columns] * student_scale)
    hidden_mine, hidden_other = group_rows((active * up_sum).astype(BF16))

    down = jnp.concatenate(
        [product(hidden_mine, student_down), product(hidden_other, student_down)], axis=0
    ).astype(BF16)
    out_rows = (student_in + sum_scatter(down, MODEL)).astype(BF16)
    student_out = spread(out_rows, MODEL)

    def gap(rows):
        added = product(teacher_hidden[rows], teacher_down)
        return product(student_out[rows], projection) - tap_scale[rows] * added

    gap_sum = group_sum(gap(slice(0, half)), gap(slice(half, tokens)))
    base = lax.dynamic_slice_in_dim(teacher_in, core * half + row_start, block, 0)
    difference = gap_sum - base.astype(F32)
    loss_part = jnp.sum(weight * difference * difference) / DT
    pred_grad = (tokens / 16 * weight * difference).astype(BF16)
    pred_mine, pred_other = group_rows(pred_grad)
    pred_all = jnp.concatenate([pred_mine, pred_other], axis=0)
    grad_proj = transpose_product(student_out, pred_all)

    out_partial = jnp.concatenate(
        [product_transposed(pred_mine, projection), product_transposed(pred_other, projection)], axis=0
    ).astype(BF16)
    loss_columns = jnp.broadcast_to(two_parts(loss_part[None]), (tokens, 2))
    second = sum_scatter(widen(out_partial, loss_columns), MODEL)
    loss_sum = jnp.broadcast_to(second[0, student_width] + second[0, student_width + 1], (8, 128))
    loss_sum = loss_sum + lax.ppermute(loss_sum, "y", [(k, k ^ 1) for k in range(4)])
    loss_sum = loss_sum + lax.ppermute(loss_sum, "y", [(k, k ^ 2) for k in range(4)])
    loss_sum = loss_sum + swap(loss_sum, "c")
    loss = 0.5 * (loss_sum + swap(loss_sum, "zh"))[0, 0]
    out_grad = spread(second[:, :student_width].astype(BF16), MODEL)
    hidden_all = jnp.concatenate([hidden_mine, hidden_other], axis=0)
    grad_down = transpose_product(hidden_all, out_grad)

    hidden_grad = group_sum(
        product_transposed(out_grad[:half], student_down),
        product_transposed(out_grad[half:], student_down),
    )
    gate_grad = hidden_grad * up_sum * slope * student_scale
    up_grad = hidden_grad * active * student_scale
    both_mine, both_other = group_rows(jnp.concatenate([gate_grad, up_grad], axis=1).astype(BF16))
    both_grad = jnp.concatenate([both_mine, both_other], axis=0)
    grad_gate = transpose_product(student_scaled, both_grad[:, :columns])
    grad_up = transpose_product(student_scaled, both_grad[:, columns:])
    return (loss, grad_gate, grad_up, grad_down, grad_proj)


def solution(mesh):
    fine = Mesh(mesh.devices.reshape(2, 4, 2, 4, 4), ("zh", "y", "c", "x", "zl"))
    placed = (
        P(),
        P(),
        P(),
        P(None, MODEL),
        P(MODEL),
        P(MODEL, GROUP),
        P(MODEL, GROUP),
        P(GROUP, MODEL),
        P(MODEL, GROUP),
        P(GROUP),
        P(GROUP, MODEL),
        P(GROUP, MODEL),
        P(MODEL, GROUP),
        P(GROUP, MODEL),
    )
    return jax.shard_map(
        shards,
        mesh=fine,
        in_specs=placed,
        out_specs=(P(), P(GROUP, MODEL), P(GROUP, MODEL), P(MODEL, GROUP), P(GROUP, MODEL)),
        check_vma=False,
    )
```

```python
import jax
import jax.numpy as jnp
from jax import lax
from jax.sharding import Mesh, PartitionSpec as P

DT = 8192
DS = 3584

EPS = 1e-06

F32 = jnp.float32
BF16 = jnp.bfloat16
GROUP = ("zh", "y", "c")
NEAR = ("y", "c")
MODEL = ("x", "zl")
SWAP = [(0, 1), (1, 0)]
LANES = 256


def silu_parts(values):
    sigmoid = jax.nn.sigmoid(values)
    return (values * sigmoid, sigmoid * (1.0 + values * (1.0 - sigmoid)))


def product(left, right):
    return jnp.dot(left, right, preferred_element_type=F32)


def transpose_product(left, right):
    return lax.dot_general(left, right, (((0,), (0,)), ((), ())), preferred_element_type=F32)


def product_transposed(left, right):
    return lax.dot_general(left, right, (((1,), (1,)), ((), ())), preferred_element_type=F32)


def swap(values, axis):
    return lax.ppermute(values, axis, SWAP)


def exchange(values, axis):
    return lax.all_to_all(values, axis, 0, 0, tiled=True)


def spread(values, axis):
    count = lax.axis_size(axis)
    copies = jnp.broadcast_to(values[None], (count,) + values.shape)
    return exchange(copies.reshape((count * values.shape[0],) + values.shape[1:]), axis)


def sum_scatter(values, axis):
    count = lax.axis_size(axis)
    parts = exchange(values, axis)
    parts = parts.reshape((count, values.shape[0] // count) + values.shape[1:])
    return jnp.sum(parts.astype(F32), axis=0)


def two_parts(values):
    high = lax.reduce_precision(values, 8, 7)
    return jnp.stack([high, values - high], axis=1).astype(BF16)


def widen(values, width, *extra):
    rows = values.shape[0]
    left = width - values.shape[1] - sum(part.shape[1] for part in extra)
    return jnp.concatenate([values, *extra, jnp.zeros((rows, left), BF16)], axis=1)


def shards(
    token_ids,
    page_ids,
    tap_layer,
    teacher_in,
    teacher_gain,
    teacher_gate,
    teacher_up,
    teacher_down,
    student_embed,
    student_gain,
    student_gate,
    student_up,
    student_down,
    projection,
):
    far = lax.axis_index("zh")
    near = lax.axis_index(NEAR)
    tokens = teacher_in.shape[0]
    half = tokens // 2
    models = lax.axis_size(MODEL)
    blocks = lax.axis_size(NEAR)
    block = half // blocks
    width = student_gain.shape[0]
    columns = student_gate.shape[1]

    def by_half(values):
        return jnp.swapaxes(values.reshape((models, 2, half // models) + values.shape[1:]), 0, 1)

    def of_half(values, which):
        rest = values.shape[1:]
        picked = lax.dynamic_index_in_dim(by_half(values), which, 0, keepdims=False)
        return picked.reshape((half,) + rest)

    def of_block(values):
        return lax.dynamic_slice_in_dim(of_half(values, far), near * block, block, 0)

    down_own = jnp.pad(student_down, ((0, 0), (0, LANES - width)))
    proj_own = jnp.pad(projection, ((0, LANES - width), (0, 0)))
    down_both = jnp.concatenate([down_own, swap(down_own, "zh")], axis=1)
    proj_both = jnp.concatenate([proj_own, swap(proj_own, "zh")], axis=0)

    pages = tap_layer.shape[0]
    member = page_ids[:, None] == jnp.arange(pages, dtype=jnp.int32)[None, :]
    counts = jnp.sum(member.astype(F32), axis=0)
    page_weight = 1.0 / (pages * counts)
    token_weight = jnp.sum(jnp.where(member, page_weight[None, :], 0.0), axis=1)
    token_tap = jnp.sum(jnp.where(member, tap_layer[None, :], 0), axis=1) == 1
    weight_half = of_half(token_weight, far)
    weight = lax.dynamic_slice_in_dim(weight_half, near * block, block, 0)[:, None]
    tap_half = of_half(jnp.where(token_tap, 1.0, 0.0), far)[:, None]
    base = of_block(teacher_in).astype(F32)

    vocab_rows = student_embed.shape[0]
    local_ids = token_ids - lax.axis_index(MODEL) * vocab_rows
    chosen = local_ids[:, None] == jnp.arange(vocab_rows, dtype=jnp.int32)[None, :]
    picked = product(chosen.astype(BF16), student_embed).astype(BF16)
    teacher_float = teacher_in.astype(F32)
    teacher_square = jnp.sum(teacher_float * teacher_float, axis=1)
    first = sum_scatter(widen(picked, LANES, two_parts(teacher_square)), MODEL)
    student_in = first[:, :width]
    teacher_total = first[:, width] + first[:, width + 1]
    student_square = jnp.sum(student_in * student_in, axis=1)
    scaled = (student_in * student_gain.astype(F32)).astype(BF16)
    student_all = spread(widen(scaled, LANES, two_parts(student_square)), MODEL)
    student_all = by_half(student_all).reshape(tokens, LANES)
    rows_here = jnp.pad(student_in, ((0, 0), (0, LANES - width))).astype(BF16)
    rows_here = rows_here.reshape(2, half // models, LANES)
    residual = jnp.concatenate(
        [
            lax.dynamic_index_in_dim(rows_here, far, 0, keepdims=False),
            swap(lax.dynamic_index_in_dim(rows_here, 1 - far, 0, keepdims=False), "zh"),
        ],
        axis=1,
    ).astype(F32)

    student_both = jnp.concatenate([student_gate, student_up], axis=1)
    depth = LANES - width
    carry = (jnp.arange(depth)[:, None] < 2) & (jnp.arange(128)[None, :] == jnp.arange(depth)[:, None])
    student_both = jnp.concatenate(
        [
            jnp.concatenate([student_both, jnp.zeros((width, 128), BF16)], axis=1),
            jnp.concatenate([jnp.zeros((depth, 2 * columns), BF16), carry.astype(BF16)], axis=1),
        ],
        axis=0,
    )
    sums = sum_scatter(product(student_all, student_both).astype(BF16), GROUP)
    student_square_sum = sums[:, 2 * columns : 2 * columns + 1] + sums[:, 2 * columns + 1 : 2 * columns + 2]
    student_scale = lax.rsqrt(student_square_sum / DS + EPS)
    up_sum = sums[:, columns : 2 * columns] * student_scale
    active, slope = silu_parts(sums[:, :columns] * student_scale)
    hidden = spread((active * up_sum).astype(BF16), NEAR)

    hidden_width = teacher_gate.shape[1]
    teacher_scaled = (teacher_float * teacher_gain.astype(F32)).astype(BF16)
    teacher_both = jnp.concatenate([teacher_gate, teacher_up], axis=1)
    teacher_partial = product(teacher_scaled, teacher_both).astype(BF16)
    teacher_sums = sum_scatter(sum_scatter(teacher_partial, "x").astype(BF16), "zl")
    teacher_scale = lax.rsqrt(teacher_total / DT + EPS)[:, None]
    teacher_active, _ = silu_parts(teacher_sums[:, :hidden_width] * teacher_scale)
    teacher_share = (teacher_active * (teacher_sums[:, hidden_width:] * teacher_scale)).astype(BF16)
    teacher_hidden = spread(spread(teacher_share, "zl"), "x")
    added = product(of_half(teacher_hidden, far), teacher_down)
    added = added + swap(
        product(of_half(teacher_hidden, 1 - far), teacher_down).astype(BF16), "zh"
    ).astype(F32)

    out_sum = sum_scatter(product(hidden, down_both).astype(BF16), MODEL)
    student_out = spread((residual + out_sum).astype(BF16), MODEL)

    gap = product(student_out, proj_both) - tap_half * added
    difference = sum_scatter(gap.astype(BF16), NEAR) - base
    pred_grad = (tokens / 16 * weight * difference).astype(BF16)
    pred = spread(pred_grad, NEAR)
    grad_proj = transpose_product(student_out[:, :width], pred) + swap(
        transpose_product(student_out[:, LANES : LANES + width], pred).astype(BF16), "zh"
    ).astype(F32)

    pred_float = pred.astype(F32)
    token_loss = jnp.sum(pred_float * pred_float, axis=1) / ((tokens / 16) ** 2 * DT * weight_half)
    out_partial = product_transposed(pred, proj_both).astype(BF16)
    spare = jnp.concatenate([out_partial[:, : 2 * LANES - 2], two_parts(token_loss)], axis=1)
    second = sum_scatter(spare, MODEL)
    loss_rows = two_parts(second[:, -2] + second[:, -1])
    out_grad = spread(jnp.concatenate([second[:, :-2].astype(BF16), loss_rows], axis=1), MODEL)
    half_loss = two_parts(jnp.sum(out_grad[:, -2:].astype(F32))[None])
    down_far = transpose_product(hidden, out_grad[:, LANES : LANES + width]).astype(BF16)
    down_far = widen(down_far, LANES, jnp.broadcast_to(half_loss, (down_far.shape[0], 2)))
    down_swapped = swap(down_far, "zh").astype(F32)
    grad_down = transpose_product(hidden, out_grad[:, :width]) + down_swapped[:, :width]
    own_loss = half_loss[0, 0].astype(F32) + half_loss[0, 1].astype(F32)
    loss = own_loss + (down_swapped[0, width] + down_swapped[0, width + 1])

    hidden_grad = sum_scatter(product_transposed(out_grad, down_both).astype(BF16), NEAR)
    gate_grad = hidden_grad * up_sum * slope * student_scale
    up_grad = hidden_grad * active * student_scale
    both_near = jnp.concatenate([gate_grad, up_grad], axis=1).astype(BF16)
    both_far = swap(both_near, "zh")
    student_rows = student_all.reshape(2, blocks // 2, 2, block, LANES)[..., :width]

    def grads(both, which):
        own = spread(both, "y")
        every = jnp.concatenate([own, swap(own, "c")], axis=0)
        rows = lax.dynamic_index_in_dim(student_rows, which, 0, keepdims=False)
        core = lax.axis_index("c")
        rows = jnp.concatenate(
            [lax.dynamic_index_in_dim(rows, k, 1, keepdims=False) for k in (core, 1 - core)], axis=0
        ).reshape(half, width)
        return (
            transpose_product(rows, every[:, :columns]),
            transpose_product(rows, every[:, columns:]),
        )

    gate_first, up_first = grads(both_near, far)
    gate_second, up_second = grads(both_far, 1 - far)
    return (loss, gate_first + gate_second, up_first + up_second, grad_down, grad_proj)


def solution(mesh):
    fine = Mesh(mesh.devices.reshape(2, 4, 2, 4, 4), ("zh", "y", "c", "x", "zl"))
    placed = (
        P(),
        P(),
        P(),
        P(None, MODEL),
        P(MODEL),
        P(MODEL, GROUP),
        P(MODEL, GROUP),
        P(GROUP, MODEL),
        P(MODEL, GROUP),
        P(GROUP),
        P(GROUP, MODEL),
        P(GROUP, MODEL),
        P(MODEL, GROUP),
        P(GROUP, MODEL),
    )
    return jax.shard_map(
        shards,
        mesh=fine,
        in_specs=placed,
        out_specs=(P(), P(GROUP, MODEL), P(GROUP, MODEL), P(MODEL, GROUP), P(GROUP, MODEL)),
        check_vma=False,
    )
```

```python
import jax
import jax.numpy as jnp
from jax import lax
from jax.sharding import Mesh, PartitionSpec as P

DT = 8192
DS = 3584

EPS = 1e-06

F32 = jnp.float32
BF16 = jnp.bfloat16
GROUP = ("zh", "y", "c")
MODEL = ("x", "zl")
SWAP = [(0, 1), (1, 0)]
LANES = 256
PAIRS = {step: [(at, at ^ step) for at in range(4)] for step in (1, 2, 3)}


def silu_parts(values):
    sigmoid = jax.nn.sigmoid(values)
    return (values * sigmoid, sigmoid * (1.0 + values * (1.0 - sigmoid)))


def product(left, right):
    return jnp.dot(left, right, preferred_element_type=F32)


def transpose_product(left, right):
    return lax.dot_general(left, right, (((0,), (0,)), ((), ())), preferred_element_type=F32)


def product_transposed(left, right):
    return lax.dot_general(left, right, (((1,), (1,)), ((), ())), preferred_element_type=F32)


def swap(values, axis):
    return lax.ppermute(values, axis, SWAP)


def exchange(values, axis):
    return lax.all_to_all(values, axis, 0, 0, tiled=True)


def copies(values, axis):
    count = lax.axis_size(axis)
    many = jnp.broadcast_to(values[None], (count,) + values.shape)
    return many.reshape((count * values.shape[0],) + values.shape[1:])


def spread(values, axis):
    return exchange(copies(values, axis), axis)


def sum_scatter(values, axis):
    count = lax.axis_size(axis)
    parts = exchange(values, axis)
    parts = parts.reshape((count, values.shape[0] // count) + values.shape[1:])
    return jnp.sum(parts.astype(F32), axis=0)


def group_sum(mine, other):
    received = swap(other.astype(BF16), "c")
    pair = (mine + received.astype(F32)).astype(BF16)
    total = lax.reduce_precision(sum_scatter(pair, "y"), 8, 7)
    return total + swap(total.astype(BF16), "zh").astype(F32)


def group_rows(values):
    mine = spread(values, "y")
    return mine, swap(mine, "c")


def after(values, earlier):
    return lax.optimization_barrier((values, earlier))[0]


def with_parts(values, column, place):
    high = lax.reduce_precision(column, 8, 7)
    at = lax.broadcasted_iota(jnp.int32, values.shape, 1)
    spare = jnp.where(at == place, high, column - high)
    return jnp.where((at == place) | (at == place + 1), spare, values).astype(BF16)


def column_sum(values, place):
    return values[:, place : place + 1] + values[:, place + 1 : place + 2]


def shards(
    token_ids,
    page_ids,
    tap_layer,
    teacher_in,
    teacher_gain,
    teacher_gate,
    teacher_up,
    teacher_down,
    student_embed,
    student_gain,
    student_gate,
    student_up,
    student_down,
    projection,
):
    core = lax.axis_index("c")
    tokens, teacher_width = teacher_in.shape
    half = tokens // 2
    block = half // lax.axis_size("y")
    student_width = student_gain.shape[0]

    def halves_first(values):
        turned = jnp.concatenate([values[half:], values[:half]], axis=0)
        return jnp.where(core == 0, values, turned)

    def rows_at(values, start, count):
        return lax.dynamic_slice_in_dim(values, start, count, 0)

    row_start = lax.axis_index("y") * block

    pages = tap_layer.shape[0]
    member = page_ids[:, None] == jnp.arange(pages, dtype=jnp.int32)[None, :]
    counts = jnp.sum(member.astype(F32), axis=0)
    page_weight = 1.0 / (pages * counts)
    token_weight = jnp.sum(jnp.where(member, page_weight[None, :], 0.0), axis=1, keepdims=True)
    token_tap = jnp.sum(jnp.where(member, tap_layer[None, :], 0), axis=1, keepdims=True)
    weight = rows_at(token_weight, core * half + row_start, block)

    vocab_rows = student_embed.shape[0]
    local_ids = token_ids - lax.axis_index(MODEL) * vocab_rows
    chosen = local_ids[:, None] == jnp.arange(vocab_rows, dtype=jnp.int32)[None, :]
    picked = product(chosen.astype(BF16), student_embed).astype(BF16)
    teacher_square = jnp.sum(jnp.square(teacher_in.astype(F32)), axis=1, keepdims=True)
    spare = LANES - student_width
    picked = jnp.pad(picked, ((0, 0), (0, spare)))
    payload = halves_first(with_parts(picked.astype(F32), teacher_square, student_width))
    first = sum_scatter(payload, MODEL)

    teacher_scaled = after(teacher_in, payload).astype(F32) * teacher_gain.astype(F32)
    teacher_scaled = halves_first(teacher_scaled.astype(BF16))
    teacher_both = jnp.concatenate([teacher_gate, teacher_up], axis=1)
    teacher_partial = product(teacher_scaled, teacher_both).astype(BF16)
    gain = jnp.pad(student_gain, (0, spare)).astype(F32)
    down_wide = jnp.pad(after(student_down, payload), ((0, 0), (0, spare)))
    proj_wide = jnp.pad(after(projection, payload), ((0, spare), (0, 0)))
    first = after(first, (teacher_partial, down_wide, proj_wide))
    quarter = tokens // 4
    part_rows = quarter // 4
    x_at = lax.axis_index("x")
    z_at = lax.axis_index("zl")

    def x_block(which):
        return rows_at(teacher_partial, which * quarter, quarter)

    teacher_total = column_sum(first, student_width)
    student_in = jnp.where(jnp.arange(LANES) < student_width, first, 0.0)
    student_square = jnp.sum(student_in * student_in, axis=1, keepdims=True)
    share_rows = with_parts(student_in * gain, student_square, student_width)
    teacher_partial = after(teacher_partial, share_rows)
    sent = {step: lax.ppermute(x_block(x_at ^ step), "x", PAIRS[step]) for step in (2, 1, 3)}
    student_all = spread(share_rows, MODEL)
    student_scaled = student_all[:, :student_width]

    columns = student_gate.shape[1]
    student_both = jnp.concatenate([student_gate, student_up], axis=1)
    depth = spare
    carry = (jnp.arange(depth)[:, None] < 2) & (jnp.arange(128)[None, :] == jnp.arange(depth)[:, None])
    student_both = jnp.concatenate(
        [
            jnp.concatenate([student_both, jnp.zeros((student_width, 128), BF16)], axis=1),
            jnp.concatenate([jnp.zeros((depth, 2 * columns), BF16), carry.astype(BF16)], axis=1),
        ],
        axis=0,
    )
    sums_other = swap(product(student_all[half:], student_both).astype(BF16), "c")
    pair = (product(student_all[:half], student_both) + sums_other.astype(F32)).astype(BF16)
    x_sums = x_block(x_at).astype(F32) + after(sent[2], pair).astype(F32)
    pair = after(pair, x_sums)
    y_sums = sum_scatter(pair, "y")
    x_sums = x_sums + after(sent[1], y_sums).astype(F32)
    y_sums = after(y_sums, x_sums)
    sums = y_sums + swap(y_sums.astype(BF16), "zh").astype(F32)
    student_scale = lax.rsqrt(column_sum(sums, 2 * columns) / DS + EPS)
    up_sum = sums[:, columns : 2 * columns] * student_scale
    active, slope = silu_parts(sums[:, :columns] * student_scale)
    hidden_share = (active * up_sum).astype(BF16)
    hidden_copies = copies(hidden_share, "y")
    hidden_mine = exchange(hidden_copies, "y")
    hidden_other = swap(hidden_mine, "c")

    hidden_width = teacher_gate.shape[1]
    x_sums = x_sums + after(sent[3], hidden_copies).astype(F32)
    arrived = [
        lax.ppermute(
            rows_at(x_sums, (z_at ^ step) * part_rows, part_rows).astype(BF16), "zl", PAIRS[step]
        )
        for step in (3, 2, 1)
    ]
    down = jnp.concatenate(
        [product(hidden_mine, down_wide), product(hidden_other, down_wide)], axis=0
    ).astype(BF16)
    teacher_sums = rows_at(x_sums, z_at * part_rows, part_rows)
    for part in after(arrived, down):
        teacher_sums = teacher_sums + part.astype(F32)
    teacher_scale = lax.rsqrt(teacher_total / DT + EPS)
    teacher_active, _ = silu_parts(teacher_sums[:, :hidden_width] * teacher_scale)
    teacher_share = (teacher_active * (teacher_sums[:, hidden_width:] * teacher_scale)).astype(BF16)
    arrived = [lax.ppermute(teacher_share, "zl", PAIRS[step]) for step in (1, 2, 3)]

    out_rows = (student_in + sum_scatter(down, MODEL)).astype(BF16)
    out_copies = copies(out_rows, MODEL)
    z_all = jnp.concatenate([teacher_share] + after(arrived, out_copies), axis=0)
    arrived = [lax.ppermute(z_all, "x", PAIRS[step]) for step in (1, 2, 3)]
    student_out = exchange(out_copies, MODEL)
    teacher_held = jnp.concatenate([z_all] + after(arrived, student_out), axis=0)

    held = jnp.arange(tokens, dtype=jnp.int32)
    held_model = ((held // quarter) ^ x_at) * 4 + ((held // part_rows % 4) ^ z_at)
    held_token = held_model * part_rows + held % part_rows
    order = (held[:, None] == held_token[None, :]) & (halves_first(token_tap) == 1)
    teacher_hidden = product(order.astype(BF16), teacher_held).astype(BF16)

    def gap(rows):
        added = product(teacher_hidden[rows], teacher_down)
        return product(student_out[rows], proj_wide) - added

    gap_sum = group_sum(gap(slice(0, half)), gap(slice(half, tokens)))
    base = rows_at(teacher_in, core * half + row_start, block)
    difference = gap_sum - base.astype(F32)
    pred_grad = (tokens / 16 * weight * difference).astype(BF16)
    pred_mine, pred_other = group_rows(pred_grad)
    pred_all = jnp.concatenate([pred_mine, pred_other], axis=0)
    grad_proj = transpose_product(student_out[:, :student_width], pred_all)

    pred_float = pred_all.astype(F32)
    token_loss = jnp.sum(pred_float * pred_float, axis=1, keepdims=True)
    token_loss = token_loss / ((tokens / 16) ** 2 * DT * halves_first(token_weight))
    out_partial = with_parts(product_transposed(pred_all, proj_wide), token_loss, student_width)
    second = sum_scatter(out_partial, MODEL)
    out_all = spread(with_parts(second, column_sum(second, student_width), student_width), MODEL)
    out_grad = out_all[:, :student_width]
    loss_terms = column_sum(out_all.astype(F32), student_width)
    loss_halves = jnp.sum(loss_terms.reshape(2, half), axis=1)
    loss = loss_halves[0] + loss_halves[1]
    hidden_all = jnp.concatenate([hidden_mine, hidden_other], axis=0)
    grad_down = transpose_product(hidden_all, out_grad)

    hidden_grad = group_sum(
        product_transposed(out_all[:half], down_wide), product_transposed(out_all[half:], down_wide)
    )
    gate_grad = hidden_grad * up_sum * slope * student_scale
    up_grad = hidden_grad * active * student_scale
    both_mine, both_other = group_rows(jnp.concatenate([gate_grad, up_grad], axis=1).astype(BF16))
    mine_scaled, other_scaled = student_scaled[:half], student_scaled[half:]

    def weight_grad(part):
        return transpose_product(mine_scaled, both_mine[:, part]) + transpose_product(
            other_scaled, both_other[:, part]
        )

    grad_gate = weight_grad(slice(0, columns))
    grad_up = weight_grad(slice(columns, 2 * columns))
    return (loss, grad_gate, grad_up, grad_down, grad_proj)


def solution(mesh):
    fine = Mesh(mesh.devices.reshape(2, 4, 2, 4, 4), ("zh", "y", "c", "x", "zl"))
    placed = (
        P(),
        P(),
        P(),
        P(None, MODEL),
        P(MODEL),
        P(MODEL, GROUP),
        P(MODEL, GROUP),
        P(GROUP, MODEL),
        P(MODEL, GROUP),
        P(GROUP),
        P(GROUP, MODEL),
        P(GROUP, MODEL),
        P(MODEL, GROUP),
        P(GROUP, MODEL),
    )
    return jax.shard_map(
        shards,
        mesh=fine,
        in_specs=placed,
        out_specs=(P(), P(GROUP, MODEL), P(GROUP, MODEL), P(MODEL, GROUP), P(GROUP, MODEL)),
        check_vma=False,
    )
```

```python
import jax
import jax.numpy as jnp
from jax import lax
from jax.sharding import Mesh, PartitionSpec as P

DT = 8192
DS = 3584

EPS = 1e-06

F32 = jnp.float32
BF16 = jnp.bfloat16
GROUP = ("zh", "y", "c")
MODEL = ("x", "zl")
SWAP = [(0, 1), (1, 0)]
LANES = 256
PAIRS = {step: [(at, at ^ step) for at in range(4)] for step in (1, 2, 3)}


def silu_parts(values):
    sigmoid = jax.nn.sigmoid(values)
    return (values * sigmoid, sigmoid * (1.0 + values * (1.0 - sigmoid)))


def product(left, right):
    return jnp.dot(left, right, preferred_element_type=F32)


def transpose_product(left, right):
    return lax.dot_general(left, right, (((0,), (0,)), ((), ())), preferred_element_type=F32)


def product_transposed(left, right):
    return lax.dot_general(left, right, (((1,), (1,)), ((), ())), preferred_element_type=F32)


def swap(values, axis):
    return lax.ppermute(values, axis, SWAP)


def exchange(values, axis):
    return lax.all_to_all(values, axis, 0, 0, tiled=True)


def copies(values, axis):
    count = lax.axis_size(axis)
    many = jnp.broadcast_to(values[None], (count,) + values.shape)
    return many.reshape((count * values.shape[0],) + values.shape[1:])


def spread(values, axis):
    return exchange(copies(values, axis), axis)


def sum_scatter(values, axis):
    count = lax.axis_size(axis)
    parts = exchange(values, axis)
    parts = parts.reshape((count, values.shape[0] // count) + values.shape[1:])
    return jnp.sum(parts.astype(F32), axis=0)


def pair_sum(values):
    values = lax.reduce_precision(values, 8, 7)
    return values + swap(values.astype(BF16), "zh").astype(F32)


def after(values, earlier):
    return lax.optimization_barrier((values, earlier))[0]


def with_parts(values, column, place):
    high = lax.reduce_precision(column, 8, 7)
    at = lax.broadcasted_iota(jnp.int32, values.shape, 1)
    spare = jnp.where(at == place, high, column - high)
    return jnp.where((at == place) | (at == place + 1), spare, values).astype(BF16)


def column_sum(values, place):
    return values[:, place : place + 1] + values[:, place + 1 : place + 2]


def shards(
    token_ids,
    page_ids,
    tap_layer,
    teacher_in,
    teacher_gain,
    teacher_gate,
    teacher_up,
    teacher_down,
    student_embed,
    student_gain,
    student_gate,
    student_up,
    student_down,
    projection,
):
    core = lax.axis_index("c")
    x_at = lax.axis_index("x")
    z_at = lax.axis_index("zl")
    tokens = teacher_in.shape[0]
    half = tokens // 2
    models = lax.axis_size(MODEL)
    share = half // models
    block = half // lax.axis_size("y")
    width = student_gain.shape[0]
    columns = student_gate.shape[1]
    spare = LANES - width
    place = width

    def rows_at(values, start, count):
        return lax.dynamic_slice_in_dim(values, start, count, 0)

    def by_model(values):
        parts = values.reshape(2, models, share, values.shape[1])
        return jnp.swapaxes(parts, 0, 1).reshape(values.shape)

    def of_core(values, which):
        return rows_at(values, which * share, share)

    def both_cores(values, axis):
        return jnp.concatenate([values, swap(values, "c")], axis=axis)

    pages = tap_layer.shape[0]
    member = page_ids[:, None] == jnp.arange(pages, dtype=jnp.int32)[None, :]
    counts = jnp.sum(member.astype(F32), axis=0)
    page_weight = 1.0 / (pages * counts)
    token_weight = jnp.sum(jnp.where(member, page_weight[None, :], 0.0), axis=1, keepdims=True)
    token_tap = jnp.sum(jnp.where(member, tap_layer[None, :], 0), axis=1, keepdims=True)
    weight_half = rows_at(token_weight, core * half, half)
    row_start = core * half + lax.axis_index("y") * block
    weight = rows_at(token_weight, row_start, block)
    base = rows_at(teacher_in, row_start, block)

    vocab_rows = student_embed.shape[0]
    local_ids = token_ids - lax.axis_index(MODEL) * vocab_rows
    chosen = local_ids[:, None] == jnp.arange(vocab_rows, dtype=jnp.int32)[None, :]
    picked = product(chosen.astype(BF16), student_embed).astype(BF16)
    teacher_square = jnp.sum(jnp.square(teacher_in.astype(F32)), axis=1, keepdims=True)
    picked = jnp.pad(picked, ((0, 0), (0, spare)))
    payload = by_model(with_parts(picked.astype(F32), teacher_square, place))
    first = sum_scatter(payload, MODEL)

    teacher_scaled = by_model(after(teacher_in, payload) * teacher_gain)
    teacher_both = jnp.concatenate([teacher_gate, teacher_up], axis=1)
    teacher_partial = product(teacher_scaled, teacher_both).astype(BF16)
    x_sums = lax.psum_scatter(teacher_partial, "x", scatter_dimension=0, tiled=True)
    gain = jnp.pad(student_gain, (0, spare)).astype(F32)
    down_wide = jnp.pad(after(student_down, payload), ((0, 0), (0, spare)))
    proj_wide = jnp.pad(after(projection, payload), ((0, spare), (0, 0)))
    student_both = jnp.concatenate([student_gate, student_up], axis=1)
    carry = (jnp.arange(spare)[:, None] < 2) & (jnp.arange(128)[None, :] == jnp.arange(spare)[:, None])
    student_both = jnp.concatenate(
        [
            jnp.concatenate([student_both, jnp.zeros((width, 128), BF16)], axis=1),
            jnp.concatenate([jnp.zeros((spare, 2 * columns), BF16), carry.astype(BF16)], axis=1),
        ],
        axis=0,
    )
    first = after(first, (teacher_partial, down_wide, proj_wide, student_both))
    quarter = tokens // 4
    part_rows = quarter // 4

    teacher_total = column_sum(first, place)
    student_in = jnp.where(jnp.arange(LANES) < width, first, 0.0)
    student_square = jnp.sum(student_in * student_in, axis=1, keepdims=True)
    share_rows = with_parts(student_in * gain, student_square, place)
    both_rows = jnp.concatenate([share_rows, student_in.astype(BF16)], axis=1)
    rows_mine, rows_far = of_core(both_rows, core), swap(of_core(both_rows, 1 - core), "c")
    student_all = spread(jnp.concatenate([rows_mine[:, :LANES], rows_far[:, :LANES]], axis=1), MODEL)
    residual = jnp.concatenate([rows_mine[:, LANES:], rows_far[:, LANES:]], axis=1).astype(F32)

    weights_all = both_cores(student_both, 0)
    y_sums = sum_scatter(product(student_all, weights_all).astype(BF16), "y")
    y_sums = after(y_sums, x_sums)
    sums = y_sums + swap(y_sums.astype(BF16), "zh").astype(F32)
    student_scale = lax.rsqrt(column_sum(sums, 2 * columns) / DS + EPS)
    up_sum = sums[:, columns : 2 * columns] * student_scale
    active, slope = silu_parts(sums[:, :columns] * student_scale)
    hidden_copies = copies((active * up_sum).astype(BF16), "y")

    hidden_width = teacher_gate.shape[1]
    arrived = [
        lax.ppermute(rows_at(x_sums, (z_at ^ step) * part_rows, part_rows), "zl", PAIRS[step])
        for step in (3, 2, 1)
    ]
    teacher_sums = rows_at(x_sums, z_at * part_rows, part_rows).astype(F32)
    for part in after(arrived, hidden_copies):
        teacher_sums = teacher_sums + part.astype(F32)
    teacher_scale = lax.rsqrt(teacher_total / DT + EPS)
    teacher_active, _ = silu_parts(teacher_sums[:, :hidden_width] * teacher_scale)
    teacher_share = (teacher_active * (teacher_sums[:, hidden_width:] * teacher_scale)).astype(BF16)
    arrived = [lax.ppermute(teacher_share, "zl", PAIRS[step]) for step in (1, 2, 3)]

    hidden = exchange(hidden_copies, "y")
    down_all = both_cores(down_wide, 1)
    down = product(hidden, down_all).astype(BF16)
    z_all = jnp.concatenate([teacher_share] + arrived, axis=0)
    arrived = [lax.ppermute(z_all, "x", PAIRS[step]) for step in (1, 2, 3)]
    down = after(down, z_all)

    out_rows = (residual + sum_scatter(down, MODEL)).astype(BF16)
    student_out = spread(out_rows, MODEL)

    added_held = jnp.concatenate(
        [product(part, teacher_down).astype(BF16) for part in [z_all] + arrived], axis=0
    )
    held = jnp.arange(tokens, dtype=jnp.int32)
    held_model = ((held // quarter) ^ x_at) * 4 + ((held // part_rows % 4) ^ z_at)
    held_token = (held // share % 2) * half + held_model * share + held % share
    wanted = (held + core * half) % tokens
    tapped = jnp.concatenate(
        [rows_at(token_tap, core * half, half), rows_at(token_tap, (1 - core) * half, half)], axis=0
    )
    order = ((wanted[:, None] == held_token[None, :]) & (tapped == 1)).astype(BF16)
    added_far = swap(product(order[half:], added_held).astype(BF16), "c")
    added = product(order[:half], added_held) + added_far.astype(F32)

    proj_all = both_cores(proj_wide, 0)
    gap = (product(student_out, proj_all) - added).astype(BF16)
    difference = pair_sum(sum_scatter(gap, "y")) - base.astype(F32)
    pred_grad = (tokens / 16 * weight * difference).astype(BF16)
    pred = spread(pred_grad, "y")
    other_scaled = swap(student_all[:, LANES:], "c")[:, :width]
    pred, other_scaled = lax.optimization_barrier((pred, other_scaled))

    pred_float = pred.astype(F32)
    token_loss = jnp.sum(pred_float * pred_float, axis=1, keepdims=True)
    token_loss = token_loss / ((tokens / 16) ** 2 * DT * weight_half)
    out_partial = with_parts(product_transposed(pred, proj_all), token_loss, place)
    second = sum_scatter(out_partial, MODEL)
    out_all = spread(with_parts(second, column_sum(second, place), place), MODEL)

    far_at = slice(LANES, LANES + width)
    proj_far = swap(transpose_product(student_out[:, far_at], pred).astype(BF16), "c")
    out_all = after(out_all, proj_far)

    hidden_partial = product_transposed(out_all, down_all).astype(BF16)
    grad_proj = transpose_product(student_out[:, :width], after(pred, hidden_partial)) + proj_far.astype(F32)
    out_later = after(out_all, hidden_partial)
    at = lax.broadcasted_iota(jnp.int32, (half, LANES), 1)
    own_terms = out_later[:, place : place + 2]
    terms = jnp.where(at == place, own_terms[:, :1], jnp.where(at == place + 1, own_terms[:, 1:], 0))
    terms = jnp.pad(terms, ((0, hidden.shape[1] - half), (0, 0))).astype(F32)
    down_far = swap((transpose_product(hidden, out_later[:, LANES:]) + terms).astype(BF16), "c")
    grad_down = transpose_product(hidden, out_later[:, :width]) + down_far[:, :width].astype(F32)
    y_sums = after(sum_scatter(hidden_partial, "y"), down_far)
    hidden_grad, grad_down = lax.optimization_barrier((pair_sum(y_sums), grad_down))
    gate_grad = hidden_grad * up_sum * slope * student_scale
    up_grad = hidden_grad * active * student_scale
    both_copies = copies(jnp.concatenate([gate_grad, up_grad], axis=1).astype(BF16), "y")
    both_mine = exchange(both_copies, "y")

    loss_terms = jnp.stack([own_terms, down_far[:half, place : place + 2]])
    core_loss = jnp.sum(loss_terms.astype(F32), axis=(1, 2))
    loss = core_loss[0] + core_loss[1]
    both_mine, grad_proj, loss = lax.optimization_barrier((both_mine, grad_proj, loss))
    both_other = swap(both_mine, "c")
    parts = (slice(0, columns), slice(columns, 2 * columns))
    mine_grads = [transpose_product(student_all[:, :width], both_mine[:, part]) for part in parts]
    both_other, mine_grads = lax.optimization_barrier((both_other, mine_grads))
    grad_gate, grad_up = [
        mine + transpose_product(other_scaled, both_other[:, part]) for mine, part in zip(mine_grads, parts)
    ]
    return (loss, grad_gate, grad_up, grad_down, grad_proj)


def solution(mesh):
    fine = Mesh(mesh.devices.reshape(2, 4, 2, 4, 4), ("zh", "y", "c", "x", "zl"))
    placed = (
        P(),
        P(),
        P(),
        P(None, MODEL),
        P(MODEL),
        P(MODEL, GROUP),
        P(MODEL, GROUP),
        P(GROUP, MODEL),
        P(MODEL, GROUP),
        P(GROUP),
        P(GROUP, MODEL),
        P(GROUP, MODEL),
        P(MODEL, GROUP),
        P(GROUP, MODEL),
    )
    return jax.shard_map(
        shards,
        mesh=fine,
        in_specs=placed,
        out_specs=(P(), P(GROUP, MODEL), P(GROUP, MODEL), P(MODEL, GROUP), P(GROUP, MODEL)),
        check_vma=False,
    )
```

```python
import jax
import jax.numpy as jnp
from jax import lax
from jax.sharding import Mesh, PartitionSpec as P

DT = 8192
DS = 3584

EPS = 1e-06

F32 = jnp.float32
BF16 = jnp.bfloat16
GROUP = ("zh", "y", "c")
MODEL = ("x", "zl")
SWAP = [(0, 1), (1, 0)]
LANES = 256
PAIRS = {step: [(at, at ^ step) for at in range(4)] for step in (1, 2, 3)}


def silu_parts(values):
    sigmoid = jax.nn.sigmoid(values)
    return (values * sigmoid, sigmoid * (1.0 + values * (1.0 - sigmoid)))


def product(left, right):
    return jnp.dot(left, right, preferred_element_type=F32)


def transpose_product(left, right):
    return lax.dot_general(left, right, (((0,), (0,)), ((), ())), preferred_element_type=F32)


def product_transposed(left, right):
    return lax.dot_general(left, right, (((1,), (1,)), ((), ())), preferred_element_type=F32)


def swap(values, axis):
    return lax.ppermute(values, axis, SWAP)


def exchange(values, axis):
    return lax.all_to_all(values, axis, 0, 0, tiled=True)


def copies(values, axis):
    count = lax.axis_size(axis)
    many = jnp.broadcast_to(values[None], (count,) + values.shape)
    return many.reshape((count * values.shape[0],) + values.shape[1:])


def spread(values, axis):
    return exchange(copies(values, axis), axis)


def sum_scatter(values, axis):
    count = lax.axis_size(axis)
    parts = exchange(values, axis)
    parts = parts.reshape((count, values.shape[0] // count) + values.shape[1:])
    return jnp.sum(parts.astype(F32), axis=0)


def pair_sum(values):
    values = lax.reduce_precision(values, 8, 7)
    return values + swap(values.astype(BF16), "zh").astype(F32)


def after(values, earlier):
    return lax.optimization_barrier((values, earlier))[0]


def with_parts(values, column, place):
    high = lax.reduce_precision(column, 8, 7)
    at = lax.broadcasted_iota(jnp.int32, values.shape, 1)
    spare = jnp.where(at == place, high, column - high)
    return jnp.where((at == place) | (at == place + 1), spare, values).astype(BF16)


def column_sum(values, place):
    return values[:, place : place + 1] + values[:, place + 1 : place + 2]


def shards(
    token_ids,
    page_ids,
    tap_layer,
    teacher_in,
    teacher_gain,
    teacher_gate,
    teacher_up,
    teacher_down,
    student_embed,
    student_gain,
    student_gate,
    student_up,
    student_down,
    projection,
):
    core = lax.axis_index("c")
    x_at = lax.axis_index("x")
    z_at = lax.axis_index("zl")
    tokens = teacher_in.shape[0]
    half = tokens // 2
    models = lax.axis_size(MODEL)
    share = half // models
    block = half // lax.axis_size("y")
    width = student_gain.shape[0]
    columns = student_gate.shape[1]
    spare = LANES - width
    place = width

    def rows_at(values, start, count):
        return lax.dynamic_slice_in_dim(values, start, count, 0)

    def by_model(values):
        parts = values.reshape(2, models, share, values.shape[1])
        return jnp.swapaxes(parts, 0, 1).reshape(values.shape)

    def of_core(values, which):
        return rows_at(values, which * share, share)

    def both_cores(values, axis):
        return jnp.concatenate([values, swap(values, "c")], axis=axis)

    pages = tap_layer.shape[0]
    member = page_ids[:, None] == jnp.arange(pages, dtype=jnp.int32)[None, :]
    counts = jnp.sum(member.astype(F32), axis=0)
    page_weight = 1.0 / (pages * counts)
    token_weight = jnp.sum(jnp.where(member, page_weight[None, :], 0.0), axis=1, keepdims=True)
    token_tap = jnp.sum(jnp.where(member, tap_layer[None, :], 0), axis=1, keepdims=True)
    weight_half = rows_at(token_weight, core * half, half)
    row_start = core * half + lax.axis_index("y") * block
    weight = rows_at(token_weight, row_start, block)
    base = rows_at(teacher_in, row_start, block)

    vocab_rows = student_embed.shape[0]
    local_ids = token_ids - lax.axis_index(MODEL) * vocab_rows
    chosen = local_ids[:, None] == jnp.arange(vocab_rows, dtype=jnp.int32)[None, :]
    picked = product(chosen.astype(BF16), student_embed).astype(BF16)
    teacher_square = jnp.sum(jnp.square(teacher_in.astype(F32)), axis=1, keepdims=True)
    picked = jnp.pad(picked, ((0, 0), (0, spare)))
    payload = by_model(with_parts(picked.astype(F32), teacher_square, place))
    first = sum_scatter(payload, MODEL)

    teacher_scaled = by_model(after(teacher_in, payload) * teacher_gain)
    teacher_both = jnp.concatenate([teacher_gate, teacher_up], axis=1)
    teacher_partial = product(teacher_scaled, teacher_both).astype(BF16)
    x_sums = lax.psum_scatter(teacher_partial, "x", scatter_dimension=0, tiled=True)
    gain = jnp.pad(student_gain, (0, spare)).astype(F32)
    down_wide = jnp.pad(after(student_down, payload), ((0, 0), (0, spare)))
    proj_wide = jnp.pad(after(projection, payload), ((0, spare), (0, 0)))
    student_both = jnp.concatenate([student_gate, student_up], axis=1)
    carry = (jnp.arange(spare)[:, None] < 2) & (jnp.arange(128)[None, :] == jnp.arange(spare)[:, None])
    student_both = jnp.concatenate(
        [
            jnp.concatenate([student_both, jnp.zeros((width, 128), BF16)], axis=1),
            jnp.concatenate([jnp.zeros((spare, 2 * columns), BF16), carry.astype(BF16)], axis=1),
        ],
        axis=0,
    )
    first = after(first, (teacher_partial, down_wide, proj_wide, student_both))
    quarter = tokens // 4
    part_rows = quarter // 4

    teacher_total = column_sum(first, place)
    student_in = jnp.where(jnp.arange(LANES) < width, first, 0.0)
    student_square = jnp.sum(student_in * student_in, axis=1, keepdims=True)
    share_rows = with_parts(student_in * gain, student_square, place)
    both_rows = jnp.concatenate([share_rows, student_in.astype(BF16)], axis=1)
    rows_mine, rows_far = of_core(both_rows, core), swap(of_core(both_rows, 1 - core), "c")
    student_all = spread(jnp.concatenate([rows_mine[:, :LANES], rows_far[:, :LANES]], axis=1), MODEL)
    residual = jnp.concatenate([rows_mine[:, LANES:], rows_far[:, LANES:]], axis=1).astype(F32)

    weights_all = both_cores(student_both, 0)
    y_sums = sum_scatter(product(student_all, weights_all).astype(BF16), "y")
    y_sums = after(y_sums, x_sums)
    sums = y_sums + swap(y_sums.astype(BF16), "zh").astype(F32)
    student_scale = lax.rsqrt(column_sum(sums, 2 * columns) / DS + EPS)
    up_sum = sums[:, columns : 2 * columns] * student_scale
    active, slope = silu_parts(sums[:, :columns] * student_scale)
    hidden_copies = copies((active * up_sum).astype(BF16), "y")

    hidden_width = teacher_gate.shape[1]
    arrived = [
        lax.ppermute(rows_at(x_sums, (z_at ^ step) * part_rows, part_rows), "zl", PAIRS[step])
        for step in (3, 2, 1)
    ]
    teacher_sums = rows_at(x_sums, z_at * part_rows, part_rows).astype(F32)
    for part in after(arrived, hidden_copies):
        teacher_sums = teacher_sums + part.astype(F32)
    teacher_scale = lax.rsqrt(teacher_total / DT + EPS)
    teacher_active, _ = silu_parts(teacher_sums[:, :hidden_width] * teacher_scale)
    teacher_share = (teacher_active * (teacher_sums[:, hidden_width:] * teacher_scale)).astype(BF16)
    arrived = [lax.ppermute(teacher_share, "zl", PAIRS[step]) for step in (1, 2, 3)]

    hidden = exchange(hidden_copies, "y")
    down_all = both_cores(down_wide, 1)
    down = product(hidden, down_all).astype(BF16)
    z_all = jnp.concatenate([teacher_share] + arrived, axis=0)
    arrived = [lax.ppermute(z_all, "x", PAIRS[step]) for step in (1, 2, 3)]
    down = after(down, z_all)

    out_rows = (residual + sum_scatter(down, MODEL)).astype(BF16)
    student_out = spread(out_rows, MODEL)

    added_held = jnp.concatenate(
        [product(part, teacher_down).astype(BF16) for part in [z_all] + arrived], axis=0
    )
    held = jnp.arange(tokens, dtype=jnp.int32)
    held_model = ((held // quarter) ^ x_at) * 4 + ((held // part_rows % 4) ^ z_at)
    held_token = (held // share % 2) * half + held_model * share + held % share
    wanted = (held + core * half) % tokens
    tapped = jnp.concatenate(
        [rows_at(token_tap, core * half, half), rows_at(token_tap, (1 - core) * half, half)], axis=0
    )
    order = ((wanted[:, None] == held_token[None, :]) & (tapped == 1)).astype(BF16)
    added_far = swap(product(order[half:], added_held).astype(BF16), "c")
    added = product(order[:half], added_held) + added_far.astype(F32)

    proj_all = both_cores(proj_wide, 0)
    gap = (product(student_out, proj_all) - added).astype(BF16)
    other_scaled = swap(student_all[:, LANES:], "c")[:, :width]
    gap_sums, other_scaled = lax.optimization_barrier((sum_scatter(gap, "y"), other_scaled))
    difference = pair_sum(gap_sums) - base.astype(F32)
    pred_grad = (tokens / 16 * weight * difference).astype(BF16)
    pred = spread(pred_grad, "y")

    pred_float = pred.astype(F32)
    token_loss = jnp.sum(pred_float * pred_float, axis=1, keepdims=True)
    token_loss = token_loss / ((tokens / 16) ** 2 * DT * weight_half)
    out_partial = with_parts(product_transposed(pred, proj_all), token_loss, place)
    far_at = slice(LANES, LANES + width)
    proj_far = swap(transpose_product(student_out[:, far_at], pred).astype(BF16), "c")
    second, proj_far = lax.optimization_barrier((sum_scatter(out_partial, MODEL), proj_far))
    out_all = spread(with_parts(second, column_sum(second, place), place), MODEL)

    hidden_partial = product_transposed(out_all, down_all).astype(BF16)
    grad_proj = transpose_product(student_out[:, :width], after(pred, hidden_partial)) + proj_far.astype(F32)
    out_later = after(out_all, hidden_partial)
    at = lax.broadcasted_iota(jnp.int32, (half, LANES), 1)
    own_terms = out_later[:, place : place + 2]
    terms = jnp.where(at == place, own_terms[:, :1], jnp.where(at == place + 1, own_terms[:, 1:], 0))
    terms = jnp.pad(terms, ((0, hidden.shape[1] - half), (0, 0))).astype(F32)
    down_far = swap((transpose_product(hidden, out_later[:, LANES:]) + terms).astype(BF16), "c")
    grad_down = transpose_product(hidden, out_later[:, :width]) + down_far[:, :width].astype(F32)
    y_sums = after(sum_scatter(hidden_partial, "y"), down_far)
    hidden_grad, grad_down = lax.optimization_barrier((pair_sum(y_sums), grad_down))
    gate_grad = hidden_grad * up_sum * slope * student_scale
    up_grad = hidden_grad * active * student_scale
    both_copies = copies(jnp.concatenate([gate_grad, up_grad], axis=1).astype(BF16), "y")
    both_mine = exchange(both_copies, "y")

    loss_terms = jnp.stack([own_terms, down_far[:half, place : place + 2]])
    core_loss = jnp.sum(loss_terms.astype(F32), axis=(1, 2))
    loss = core_loss[0] + core_loss[1]
    both_mine, grad_proj, loss = lax.optimization_barrier((both_mine, grad_proj, loss))
    both_other = swap(both_mine, "c")
    parts = (slice(0, columns), slice(columns, 2 * columns))
    grad_gate, grad_up = [
        transpose_product(student_all[:, :width], both_mine[:, part])
        + transpose_product(other_scaled, both_other[:, part])
        for part in parts
    ]
    return (loss, grad_gate, grad_up, grad_down, grad_proj)


def solution(mesh):
    fine = Mesh(mesh.devices.reshape(2, 4, 2, 4, 4), ("zh", "y", "c", "x", "zl"))
    placed = (
        P(),
        P(),
        P(),
        P(None, MODEL),
        P(MODEL),
        P(MODEL, GROUP),
        P(MODEL, GROUP),
        P(GROUP, MODEL),
        P(MODEL, GROUP),
        P(GROUP),
        P(GROUP, MODEL),
        P(GROUP, MODEL),
        P(MODEL, GROUP),
        P(GROUP, MODEL),
    )
    return jax.shard_map(
        shards,
        mesh=fine,
        in_specs=placed,
        out_specs=(P(), P(GROUP, MODEL), P(GROUP, MODEL), P(MODEL, GROUP), P(GROUP, MODEL)),
        check_vma=False,
    )
```

```python
import jax
import jax.numpy as jnp
from jax import lax
from jax.sharding import Mesh, PartitionSpec as P

DT = 8192
DS = 3584

EPS = 1e-06

F32 = jnp.float32
BF16 = jnp.bfloat16
GROUP = ("zh", "y", "c")
MODEL = ("x", "zl")
SWAP = [(0, 1), (1, 0)]
LANES = 256
PAIRS = {step: [(at, at ^ step) for at in range(4)] for step in (1, 2, 3)}


def silu_parts(values):
    sigmoid = jax.nn.sigmoid(values)
    return (values * sigmoid, sigmoid * (1.0 + values * (1.0 - sigmoid)))


def product(left, right):
    return jnp.dot(left, right, preferred_element_type=F32)


def transpose_product(left, right):
    return lax.dot_general(left, right, (((0,), (0,)), ((), ())), preferred_element_type=F32)


def product_transposed(left, right):
    return lax.dot_general(left, right, (((1,), (1,)), ((), ())), preferred_element_type=F32)


def swap(values, axis):
    return lax.ppermute(values, axis, SWAP)


def exchange(values, axis):
    return lax.all_to_all(values, axis, 0, 0, tiled=True)


def copies(values, axis):
    count = lax.axis_size(axis)
    many = jnp.broadcast_to(values[None], (count,) + values.shape)
    return many.reshape((count * values.shape[0],) + values.shape[1:])


def spread(values, axis):
    return exchange(copies(values, axis), axis)


def sum_scatter(values, axis):
    count = lax.axis_size(axis)
    parts = exchange(values, axis)
    parts = parts.reshape((count, values.shape[0] // count) + values.shape[1:])
    return jnp.sum(parts.astype(F32), axis=0)


def pair_sum(values):
    values = lax.reduce_precision(values, 8, 7)
    return values + swap(values.astype(BF16), "zh").astype(F32)


def after(values, earlier):
    return lax.optimization_barrier((values, earlier))[0]


def with_parts(values, column, place):
    high = lax.reduce_precision(column, 8, 7)
    at = lax.broadcasted_iota(jnp.int32, values.shape, 1)
    spare = jnp.where(at == place, high, column - high)
    return jnp.where((at == place) | (at == place + 1), spare, values).astype(BF16)


def column_sum(values, place):
    return values[:, place : place + 1] + values[:, place + 1 : place + 2]


def shards(
    token_ids,
    page_ids,
    tap_layer,
    teacher_in,
    teacher_gain,
    teacher_gate,
    teacher_up,
    teacher_down,
    student_embed,
    student_gain,
    student_gate,
    student_up,
    student_down,
    projection,
):
    core = lax.axis_index("c")
    x_at = lax.axis_index("x")
    z_at = lax.axis_index("zl")
    tokens = teacher_in.shape[0]
    half = tokens // 2
    models = lax.axis_size(MODEL)
    share = half // models
    block = half // lax.axis_size("y")
    width = student_gain.shape[0]
    columns = student_gate.shape[1]
    spare = LANES - width
    place = width

    def rows_at(values, start, count):
        return lax.dynamic_slice_in_dim(values, start, count, 0)

    def by_model(values):
        parts = values.reshape(2, models, share, values.shape[1])
        return jnp.swapaxes(parts, 0, 1).reshape(values.shape)

    def of_core(values, which):
        return rows_at(values, which * share, share)

    def both_cores(values, axis):
        return jnp.concatenate([values, swap(values, "c")], axis=axis)

    pages = tap_layer.shape[0]
    member = page_ids[:, None] == jnp.arange(pages, dtype=jnp.int32)[None, :]
    counts = jnp.sum(member.astype(F32), axis=0)
    page_weight = 1.0 / (pages * counts)
    token_weight = jnp.sum(jnp.where(member, page_weight[None, :], 0.0), axis=1, keepdims=True)
    token_tap = jnp.sum(jnp.where(member, tap_layer[None, :], 0), axis=1, keepdims=True)
    weight_half = rows_at(token_weight, core * half, half)
    row_start = core * half + lax.axis_index("y") * block
    weight = rows_at(token_weight, row_start, block)
    base = rows_at(teacher_in, row_start, block)

    vocab_rows = student_embed.shape[0]
    local_ids = token_ids - lax.axis_index(MODEL) * vocab_rows
    chosen = local_ids[:, None] == jnp.arange(vocab_rows, dtype=jnp.int32)[None, :]
    picked = product(chosen.astype(BF16), student_embed).astype(BF16)
    teacher_square = jnp.sum(jnp.square(teacher_in.astype(F32)), axis=1, keepdims=True)
    picked = jnp.pad(picked, ((0, 0), (0, spare)))
    payload = by_model(with_parts(picked.astype(F32), teacher_square, place))
    first = sum_scatter(payload, MODEL)

    teacher_scaled = by_model(after(teacher_in, payload) * teacher_gain)
    teacher_both = jnp.concatenate([teacher_gate, teacher_up], axis=1)
    teacher_partial = product(teacher_scaled, teacher_both).astype(BF16)
    x_sums = lax.psum_scatter(teacher_partial, "x", scatter_dimension=0, tiled=True)
    gain = jnp.pad(student_gain, (0, spare)).astype(F32)
    down_wide = jnp.pad(after(student_down, payload), ((0, 0), (0, spare)))
    proj_wide = jnp.pad(after(projection, payload), ((0, spare), (0, 0)))
    student_both = jnp.concatenate([student_gate, student_up], axis=1)
    carry = (jnp.arange(spare)[:, None] < 2) & (jnp.arange(128)[None, :] == jnp.arange(spare)[:, None])
    student_both = jnp.concatenate(
        [
            jnp.concatenate([student_both, jnp.zeros((width, 128), BF16)], axis=1),
            jnp.concatenate([jnp.zeros((spare, 2 * columns), BF16), carry.astype(BF16)], axis=1),
        ],
        axis=0,
    )
    first = after(first, (teacher_partial, down_wide, proj_wide, student_both))
    quarter = tokens // 4
    part_rows = quarter // 4

    teacher_total = column_sum(first, place)
    student_in = jnp.where(jnp.arange(LANES) < width, first, 0.0)
    student_square = jnp.sum(student_in * student_in, axis=1, keepdims=True)
    share_rows = with_parts(student_in * gain, student_square, place)
    both_rows = jnp.concatenate([share_rows, student_in.astype(BF16)], axis=1)
    rows_mine, rows_far = of_core(both_rows, core), swap(of_core(both_rows, 1 - core), "c")
    student_all = spread(jnp.concatenate([rows_mine[:, :LANES], rows_far[:, :LANES]], axis=1), MODEL)
    residual = jnp.concatenate([rows_mine[:, LANES:], rows_far[:, LANES:]], axis=1).astype(F32)

    weights_all = both_cores(student_both, 0)
    y_sums = sum_scatter(product(student_all, weights_all).astype(BF16), "y")
    y_sums = after(y_sums, x_sums)
    sums = y_sums + swap(y_sums.astype(BF16), "zh").astype(F32)
    student_scale = lax.rsqrt(column_sum(sums, 2 * columns) / DS + EPS)
    up_sum = sums[:, columns : 2 * columns] * student_scale
    active, slope = silu_parts(sums[:, :columns] * student_scale)
    hidden_copies = copies((active * up_sum).astype(BF16), "y")

    hidden_width = teacher_gate.shape[1]
    arrived = [
        lax.ppermute(rows_at(x_sums, (z_at ^ step) * part_rows, part_rows), "zl", PAIRS[step])
        for step in (3, 2, 1)
    ]
    teacher_sums = rows_at(x_sums, z_at * part_rows, part_rows).astype(F32)
    for part in after(arrived, hidden_copies):
        teacher_sums = teacher_sums + part.astype(F32)
    teacher_scale = lax.rsqrt(teacher_total / DT + EPS)
    teacher_active, _ = silu_parts(teacher_sums[:, :hidden_width] * teacher_scale)
    teacher_share = (teacher_active * (teacher_sums[:, hidden_width:] * teacher_scale)).astype(BF16)
    arrived = [lax.ppermute(teacher_share, "zl", PAIRS[step]) for step in (1, 2, 3)]

    hidden = exchange(hidden_copies, "y")
    down_all = both_cores(down_wide, 1)
    down = product(hidden, down_all).astype(BF16)
    z_all = jnp.concatenate([teacher_share] + arrived, axis=0)
    arrived = [lax.ppermute(z_all, "x", PAIRS[step]) for step in (1, 2, 3)]
    down = after(down, z_all)

    out_rows = (residual + sum_scatter(down, MODEL)).astype(BF16)
    student_out = spread(out_rows, MODEL)

    added_held = jnp.concatenate(
        [product(part, teacher_down).astype(BF16) for part in [z_all] + arrived], axis=0
    )
    held = jnp.arange(tokens, dtype=jnp.int32)
    held_model = ((held // quarter) ^ x_at) * 4 + ((held // part_rows % 4) ^ z_at)
    held_token = (held // share % 2) * half + held_model * share + held % share
    wanted = (held + core * half) % tokens
    tapped = jnp.concatenate(
        [rows_at(token_tap, core * half, half), rows_at(token_tap, (1 - core) * half, half)], axis=0
    )
    order = ((wanted[:, None] == held_token[None, :]) & (tapped == 1)).astype(BF16)
    added_far = swap(product(order[half:], added_held).astype(BF16), "c")
    added = product(order[:half], added_held) + added_far.astype(F32)

    proj_all = both_cores(proj_wide, 0)
    gap = (product(student_out, proj_all) - added).astype(BF16)
    other_scaled = swap(student_all[:, LANES:], "c")[:, :width]
    gap_sums, other_scaled = lax.optimization_barrier((sum_scatter(gap, "y"), other_scaled))
    difference = pair_sum(gap_sums) - base.astype(F32)
    pred_grad = (tokens / 16 * weight * difference).astype(BF16)
    pred = spread(pred_grad, "y")

    pred_float = pred.astype(F32)
    token_loss = jnp.sum(pred_float * pred_float, axis=1, keepdims=True)
    token_loss = token_loss / ((tokens / 16) ** 2 * DT * weight_half)
    out_partial = with_parts(product_transposed(pred, proj_all), token_loss, place)
    second = sum_scatter(out_partial, MODEL)
    out_all = spread(with_parts(second, column_sum(second, place), place), MODEL)

    far_at = slice(LANES, LANES + width)
    proj_far = swap(transpose_product(student_out[:, far_at], pred).astype(BF16), "c")
    out_all = after(out_all, proj_far)

    hidden_partial = product_transposed(out_all, down_all).astype(BF16)
    grad_proj = transpose_product(student_out[:, :width], after(pred, hidden_partial)) + proj_far.astype(F32)
    out_later = after(out_all, hidden_partial)
    at = lax.broadcasted_iota(jnp.int32, (half, LANES), 1)
    own_terms = out_later[:, place : place + 2]
    terms = jnp.where(at == place, own_terms[:, :1], jnp.where(at == place + 1, own_terms[:, 1:], 0))
    terms = jnp.pad(terms, ((0, hidden.shape[1] - half), (0, 0))).astype(F32)
    down_far = swap((transpose_product(hidden, out_later[:, LANES:]) + terms).astype(BF16), "c")
    grad_down = transpose_product(hidden, out_later[:, :width]) + down_far[:, :width].astype(F32)
    y_sums = after(sum_scatter(hidden_partial, "y"), down_far)
    hidden_grad, grad_down = lax.optimization_barrier((pair_sum(y_sums), grad_down))
    gate_grad = hidden_grad * up_sum * slope * student_scale
    up_grad = hidden_grad * active * student_scale
    both_copies = copies(jnp.concatenate([gate_grad, up_grad], axis=1).astype(BF16), "y")
    both_mine = exchange(both_copies, "y")

    loss_terms = jnp.stack([own_terms, down_far[:half, place : place + 2]])
    core_loss = jnp.sum(loss_terms.astype(F32), axis=(1, 2))
    loss = core_loss[0] + core_loss[1]
    both_mine, grad_proj, loss = lax.optimization_barrier((both_mine, grad_proj, loss))
    both_other = swap(both_mine, "c")
    parts = (slice(0, columns), slice(columns, 2 * columns))
    grad_gate, grad_up = [
        transpose_product(student_all[:, :width], both_mine[:, part])
        + transpose_product(other_scaled, both_other[:, part])
        for part in parts
    ]
    return (loss, grad_gate, grad_up, grad_down, grad_proj)


def solution(mesh):
    fine = Mesh(mesh.devices.reshape(2, 4, 2, 4, 4), ("zh", "y", "c", "x", "zl"))
    placed = (
        P(),
        P(),
        P(),
        P(None, MODEL),
        P(MODEL),
        P(MODEL, GROUP),
        P(MODEL, GROUP),
        P(GROUP, MODEL),
        P(MODEL, GROUP),
        P(GROUP),
        P(GROUP, MODEL),
        P(GROUP, MODEL),
        P(MODEL, GROUP),
        P(GROUP, MODEL),
    )
    return jax.shard_map(
        shards,
        mesh=fine,
        in_specs=placed,
        out_specs=(P(), P(GROUP, MODEL), P(GROUP, MODEL), P(MODEL, GROUP), P(GROUP, MODEL)),
        check_vma=False,
    )
```
